256 devices in a mesh: dp: 64 (over x, z, core), mp: 4 (over y).
Axes of the slice: x: 4, y: 4, z: 8, core: 2. Of those that a mesh axis runs over, the one named last changes fastest.
Arguments:
- big_q: bfloat16 [40960, 2560], P('dp', 'mp'), may hold values from -5 to 5
- big_k: bfloat16 [40960, 2560], P('dp', 'mp'), may hold values from -5 to 5
- big_v: bfloat16 [40960, 2560], P('dp', 'mp'), may hold values from -6 to 6
- big_dout: bfloat16 [40960, 2560], P('dp', 'mp'), may hold values from -6 to 6
- big_counts: int32 [64, 4], P('dp'), may hold values from 1 to 320, 640 in all within a row
- small_q: bfloat16 [32768, 2560], P('dp', 'mp'), may hold values from -5 to 5
- small_k: bfloat16 [32768, 2560], P('dp', 'mp'), may hold values from -5 to 5
- small_v: bfloat16 [32768, 2560], P('dp', 'mp'), may hold values from -6 to 6
- small_image: int32 [64, 512], replicated, may hold values from 0 to 47, never falling along the last dimension, each value on 1 to 16 neighbouring positions
- owner: int32 [3072, 1], replicated, may hold values from 0 to 63; in each aligned block of 48 rows (0 to 47, 48 to 95, ...) no two rows name the same one
- owner_dout: bfloat16 [65536, 2560], P('dp', 'mp'), may hold values from -6 to 6
- reward_w: float32 [2560], P('mp'), may hold values from -1.2 to 1.2
- pair_perm: int32 [3328], replicated, may hold values from 0 to 3327, each once
Outputs:
- big_out: bfloat16 [40960, 2560], P('dp', 'mp')
- small_out: bfloat16 [65536, 2560], P('dp', 'mp')
- big_dq: bfloat16 [40960, 2560], P('dp', 'mp')
- big_dk: bfloat16 [40960, 2560], P('dp', 'mp')
- big_dv: bfloat16 [40960, 2560], P('dp', 'mp')
- small_dq: bfloat16 [32768, 2560], P('dp', 'mp')
- small_dk: bfloat16 [32768, 2560], P('dp', 'mp')
- small_dv: bfloat16 [32768, 2560], P('dp', 'mp')
- pair_loss: float32 [1664], replicated
The draws below stay inside these ranges and needn't reach their ends.
Inputs may be any that keep to these rules, and one draw needn't show every extreme that they name: `big_counts`: each row sums to 640; its largest entry is 320. `small_image`: numbers never fall along a row; every image of a row has 1 to 16 rows, and some image has exactly 16. At most 1 of the 48 small images of one device share an owner, and on some device exactly 1 do. `pair_perm`: each image number appears once.
All inputs are finite; a program needn't handle non-finite values.
Results may differ from the reference program's by a relative error of at most 0.03.
Values may be sent and summed in bfloat16 or wider, within the bound.
No kernel may reach another device: no remote copies, remote signals or barrier semaphores. Data moves between devices by JAX's collectives and lax.ppermute only.
A program may use at most 128 MiB of HBM per device.

```python
import math
import jax
import jax.numpy as jnp
import numpy as np
from jax import lax

HEADS = 20
HD = 128
BIG_ROWS = 640
BIG_IMG = 4
MIG_ROWS = 512
MIG_IMG = 48
SMALL = 16
SLOTS = 1
RECV = 1024
OWNER_ROWS = 65536
BIG_TOTAL = 40960
MIG_TOTAL = 32768
NIMG = 3328
N_DP = 64


def drawn_pair(key, pair_tag, row_count):
    features = HEADS * HD
    key = jax.random.fold_in(key, pair_tag)
    query_key, other_key = jax.random.split(key, 2)
    queries = jnp.clip(jax.random.normal(query_key, (row_count, features), jnp.float32), -4.0, 4.0)
    key_rows = jnp.clip(jax.random.normal(other_key, (row_count, features), jnp.float32), -4.0, 4.0)
    return (queries, key_rows)


def draw_big_q(key, part):
    return drawn_pair(key, 11, BIG_TOTAL)[0].astype(jnp.bfloat16)


def draw_big_k(key, part):
    return drawn_pair(key, 11, BIG_TOTAL)[1].astype(jnp.bfloat16)


def draw_small_q(key, part):
    return drawn_pair(key, 12, MIG_TOTAL)[0].astype(jnp.bfloat16)


def draw_small_k(key, part):
    return drawn_pair(key, 12, MIG_TOTAL)[1].astype(jnp.bfloat16)


def steps_of(rng, extent, cuts, least, high):
    def one(dim, parts):
        heights = jax.random.uniform(jax.random.fold_in(jax.random.fold_in(rng, 6), dim), (parts,), jnp.float32, least / len(cuts), high / len(cuts))
        return jnp.repeat(jnp.exp(heights), extent[dim] // parts).reshape((-1,) + (1,) * (len(extent) - dim - 1))

    gain = one(*cuts[0])
    for cut in cuts[1:]:
        gain = gain * one(*cut)
    return gain


def profile(number_of, total, most, lean):
    weights = [(1 << 20) // math.isqrt(grade ** lean) + 1 for grade in range(2, number_of + 1)]
    spare, counts = total - most - (number_of - 1), [1] * (number_of - 1)
    while spare > 0:
        movable = [i for i in range(number_of - 1) if counts[i] < most]
        mass, budget = sum([weights[i] for i in movable]), spare
        for i in movable:
            addition = min(most - counts[i], max(1, budget * weights[i] // mass), spare)
            counts[i] = counts[i] + addition
            spare = spare - addition
    return np.array([most] + counts)


def ragged(key, number_of, total, reach, lean):
    if number_of == 2:
        one = jax.random.randint(key, (), max(1, total - reach), min(reach, total - 1) + 1)
        return jnp.stack([one, total - one])
    tallies = jnp.asarray(profile(number_of, total, reach, lean), jnp.int32)
    twos = (number_of - 1) // 2
    source_of, taker = tallies[1:1 + 2 * twos:2], tallies[2:2 + 2 * twos:2]
    room = jnp.minimum(source_of - 1, reach - taker)
    moved = jax.random.randint(jax.random.fold_in(key, 1), (twos,), 0, 1 << 20) % (room + 1)
    tallies = tallies.at[1:1 + 2 * twos:2].set(source_of - moved).at[2:2 + 2 * twos:2].set(taker + moved)
    return tallies[jax.random.permutation(jax.random.fold_in(key, 2), number_of)]


def deal_out(rng, own, number, rows, amount, top, reach, lean):
    sequence = jax.random.permutation(rng, amount)
    packed, usual = shares(amount, rows * top, reach, lean, True), shares(amount, rows * top, reach, lean, False)
    places = jnp.arange(amount)

    def named(lengths, turn):
        used = int((lengths > 0).sum())
        fixed = max(1, used // 4)
        shifted = fixed + (places - fixed + turn * (used - fixed)) % max(1, amount - fixed)
        return jnp.zeros((amount,), jnp.int32).at[sequence[jnp.where(places < fixed, places, shifted)]].set(jnp.asarray(lengths, jnp.int32))

    lengths = jnp.where(number % 4 == 0, named(packed, number // 4), named(usual, number - number // 4 - 1))
    mixed = jax.random.permutation(jax.random.fold_in(own, 3), amount)
    donor, sink = mixed[0:amount // 2 * 2:2], mixed[1:amount // 2 * 2:2]
    room = jnp.minimum(lengths[donor] - 1, reach - lengths[sink]) // 2
    room = jnp.where((donor == sequence[0]) | (sink == sequence[0]) | (lengths[sink] == 0), 0, jnp.maximum(room, 0))
    shifted = jax.random.randint(jax.random.fold_in(own, 4), (amount // 2,), 0, 1 << 20) % (room + 1)
    lengths = lengths.at[donor].add(-shifted).at[sink].add(shifted)
    members = jnp.searchsorted(jnp.cumsum(lengths), jnp.arange(rows * top), side="right").astype(jnp.int32)
    grid = members.reshape(top, rows).T
    grid = grid[jax.random.permutation(jax.random.fold_in(own, 1), rows)]
    turn = jax.random.randint(jax.random.fold_in(own, 2), (rows, 1), 0, top)
    return jnp.take_along_axis(grid, (jnp.arange(top)[None, :] + turn) % top, axis=1)


def shares(amount, total, most, slope, full):
    weights = [(1 << 20) // math.isqrt(standing ** slope) + 1 for standing in range(1, amount + 1)]
    largest = most if full else min(most, max(-(-total // amount), total * weights[0] // sum(weights)))
    least = 1 if total - largest >= amount - 1 else 0
    holding, spare = [largest] + [least] * (amount - 1), total - largest - least * (amount - 1)
    while spare > 0:
        candidates = [i for i in range(1, amount) if holding[i] < largest] or [i for i in range(1, amount) if holding[i] < most]
        whole, left = sum([weights[i] for i in candidates]), spare
        for i in candidates:
            more = min(most - holding[i], max(1, left * weights[i] // whole), spare)
            holding[i] = holding[i] + more
            spare = spare - more
    return np.array(holding)


def bell_draw(key, extent, spread, reach, pieces=(), kind=jnp.bfloat16):
    values = jax.random.normal(key, extent, jnp.float32) * spread
    if len(pieces) > 0:
        values = steps_of(key, extent, pieces, -0.22, 0.18) * values
    return jnp.clip(values, min=-reach, max=reach).astype(kind)


def setup_inputs(seed: int = 0) -> dict:
    key_of = jax.random.split(jax.random.key(seed), 14)
    big_q = draw_big_q(jax.random.fold_in(key_of[13], 71), 0)
    big_k = draw_big_k(jax.random.fold_in(key_of[13], 71), 0)
    big_v = bell_draw(key_of[2], (BIG_TOTAL, HEADS * HD), 1.0, 6.0, ((0, 64), (1, 4)))
    big_dout = bell_draw(key_of[3], (BIG_TOTAL, HEADS * HD), 1.0, 6.0, ((0, 64), (1, 4)))
    big_counts = jax.vmap(lambda own: ragged(own, BIG_IMG, BIG_ROWS, BIG_ROWS // 2, 2))(jax.random.split(key_of[4], N_DP)).reshape((N_DP, BIG_IMG)).astype(jnp.int32)
    small_q = draw_small_q(jax.random.fold_in(key_of[13], 71), 0)
    small_k = draw_small_k(jax.random.fold_in(key_of[13], 71), 0)
    small_v = bell_draw(key_of[7], (MIG_TOTAL, HEADS * HD), 1.0, 6.0, ((0, 64), (1, 4)))
    small_image = jax.vmap(lambda own: jnp.searchsorted(jnp.cumsum(ragged(own, MIG_IMG, MIG_ROWS, SMALL, 1)), jnp.arange(MIG_ROWS), side="right"))(jax.random.split(key_of[8], N_DP)).reshape((N_DP, MIG_ROWS)).astype(jnp.int32)
    owner_keys = jax.random.split(jax.random.fold_in(key_of[9], 1), (N_DP * MIG_IMG) // MIG_IMG)
    owner_turns = jax.random.permutation(jax.random.fold_in(key_of[9], 3), (N_DP * MIG_IMG) // MIG_IMG)
    owner = jax.vmap(lambda own, number: deal_out(jax.random.fold_in(key_of[9], 2), own, number, MIG_IMG, N_DP, 1, SLOTS, 2))(owner_keys, owner_turns).reshape((N_DP * MIG_IMG, 1))
    owner_dout = bell_draw(key_of[10], (OWNER_ROWS, HEADS * HD), 1.0, 6.0, ((0, 64), (1, 4)))
    reward_w = bell_draw(key_of[11], (HEADS * HD,), 0.3, 1.2, ((0, 4),), jnp.float32)
    pair_perm = jax.random.permutation(key_of[12], NIMG).astype(jnp.int32)
    return dict(big_q=big_q, big_k=big_k, big_v=big_v, big_dout=big_dout, big_counts=big_counts, small_q=small_q, small_k=small_k, small_v=small_v, small_image=small_image, owner=owner, owner_dout=owner_dout, reward_w=reward_w, pair_perm=pair_perm)


def probabilities(queries, key_rows, allowed):
    score_scale = 1.0 / math.sqrt(HD)
    raw_scores = jnp.einsum('gqhd,gkhd->ghqk', queries.astype(jnp.float32), key_rows.astype(jnp.float32)) * score_scale
    raw_scores = jnp.where(allowed[:, None], raw_scores, -1e+30)
    row_max = lax.optimization_barrier(jnp.max(raw_scores, axis=-1, keepdims=True))
    expon = jnp.exp(raw_scores - row_max)
    row_total = lax.optimization_barrier(jnp.sum(expon, axis=-1, keepdims=True))
    return jnp.where(allowed[:, None], expon / row_total, 0.0).astype(jnp.bfloat16)

def attend(weights, values):
    return jnp.einsum('ghqk,gkhd->gqhd', weights.astype(jnp.float32), values.astype(jnp.float32)).astype(jnp.bfloat16)

def gradients(queries, key_rows, values, weights, cotangent):
    score_scale = 1.0 / math.sqrt(HD)
    prob_rows = weights.astype(jnp.float32)
    prob_grad = jnp.einsum('gqhd,gkhd->ghqk', cotangent.astype(jnp.float32), values.astype(jnp.float32))
    row_dot = lax.optimization_barrier(jnp.sum(prob_rows * prob_grad, axis=-1, keepdims=True))
    dscore = (prob_rows * (prob_grad - row_dot)).astype(jnp.bfloat16)
    value_grad = jnp.einsum('ghqk,gqhd->gkhd', prob_rows, cotangent.astype(jnp.float32)).astype(jnp.bfloat16)
    query_grad = (jnp.einsum('ghqk,gkhd->gqhd', dscore.astype(jnp.float32), key_rows.astype(jnp.float32)) * score_scale).astype(jnp.bfloat16)
    key_grad = (jnp.einsum('ghqk,gqhd->gkhd', dscore.astype(jnp.float32), queries.astype(jnp.float32)) * score_scale).astype(jnp.bfloat16)
    return (query_grad, key_grad, value_grad)

def big_forward(device_items):
    queries, key_rows, values, segment = device_items
    allowed = (segment[:, None] == segment[None, :])[None]
    weights = probabilities(queries[None], key_rows[None], allowed)
    return attend(weights, values[None])[0]

def big_backward(device_items):
    queries, key_rows, values, segment, cotangent = device_items
    allowed = (segment[:, None] == segment[None, :])[None]
    weights = probabilities(queries[None], key_rows[None], allowed)
    query_grad, key_grad, value_grad = gradients(queries[None], key_rows[None], values[None], weights, cotangent[None])
    return (query_grad[0], key_grad[0], value_grad[0])

def reference(big_q, big_k, big_v, big_dout, big_counts, small_q, small_k, small_v, small_image, owner, owner_dout, reward_w, pair_perm):
    features = HEADS * HD
    big_shape = (N_DP, BIG_ROWS, HEADS, HD)
    row_index = jnp.arange(BIG_ROWS, dtype=jnp.int32)
    big_ends = jnp.cumsum(big_counts, axis=1).astype(jnp.int32)
    starts = (big_ends - big_counts).astype(jnp.int32)
    big_seg = lax.optimization_barrier(jnp.sum((row_index[None, :, None] >= big_ends[:, None, :]).astype(jnp.int32), axis=2)).astype(jnp.int32)
    big_class = jnp.any(row_index[None, :, None] == starts[:, None, :], axis=2)
    big_queries = big_q.reshape(big_shape)
    big_keys = big_k.reshape(big_shape)
    big_values = big_v.reshape(big_shape)
    images = jnp.arange(MIG_IMG, dtype=jnp.int32)
    slot_steps = jnp.arange(SMALL, dtype=jnp.int32)
    devices = jnp.arange(N_DP, dtype=jnp.int32)
    small_count = lax.optimization_barrier(jnp.sum((small_image[:, :, None] == images).astype(jnp.int32), axis=1)).astype(jnp.int32)
    small_start = lax.optimization_barrier(jnp.sum((small_image[:, :, None] < images).astype(jnp.int32), axis=1)).astype(jnp.int32)
    owners = owner.reshape(N_DP, MIG_IMG)
    before = images[None, :] < images[:, None]
    slot_rank = lax.optimization_barrier(jnp.sum(((owners[:, :, None] == owners[:, None, :]) & before[None]).astype(jnp.int32), axis=2)).astype(jnp.int32)
    slot_base = (owners * RECV + (devices[:, None] * SLOTS + slot_rank) * SMALL).astype(jnp.int32)
    slot_dest = (slot_base[:, :, None] + slot_steps).reshape(-1).astype(jnp.int32)
    is_live = slot_steps[None, None, :] < small_count[:, :, None]
    source = (devices[:, None, None] * MIG_ROWS + small_start[:, :, None] + slot_steps).astype(jnp.int32)
    gather_at = jnp.where(is_live, source, 0).reshape(-1).astype(jnp.int32)
    scatter_at = jnp.where(is_live, source, N_DP * MIG_ROWS).reshape(-1).astype(jnp.int32)
    groups = N_DP * MIG_IMG
    live_flat = is_live.reshape(-1)

    def padded(source_rows):
        picked = source_rows.reshape(N_DP * MIG_ROWS, HEADS, HD)[gather_at]
        return jnp.where(live_flat[:, None, None], picked, 0).reshape(groups, SMALL, HEADS, HD)
    small_queries = padded(small_q)
    small_keys = padded(small_k)
    small_values = padded(small_v)
    live_rows = is_live.reshape(groups, SMALL)
    small_allowed = live_rows[:, :, None] & live_rows[:, None, :]
    small_weights = probabilities(small_queries, small_keys, small_allowed)
    small_rows_out = attend(small_weights, small_values)
    big_rows_out = lax.map(big_forward, (big_queries, big_keys, big_values, big_seg))
    weight = reward_w.astype(jnp.float32)
    big_flat = big_rows_out.reshape(N_DP, BIG_ROWS, features).astype(jnp.float32)
    big_class_rows = jnp.take_along_axis(big_flat, starts[:, :, None], axis=1)
    big_scores = lax.optimization_barrier(jnp.sum(big_class_rows * weight, axis=-1))
    small_scores = lax.optimization_barrier(jnp.sum(small_rows_out[:, 0].reshape(groups, features).astype(jnp.float32) * weight, axis=-1))
    scores = jnp.concatenate([big_scores.reshape(-1), small_scores])
    preferred = pair_perm[0::2]
    rejected = pair_perm[1::2]
    margin = scores[rejected] - scores[preferred]
    pair_loss = jax.nn.softplus(margin)
    pull_back = jax.nn.sigmoid(margin)
    image_gain = jnp.zeros((NIMG,), jnp.float32).at[preferred].set(-pull_back).at[rejected].set(pull_back)
    big_gain = image_gain[:N_DP * BIG_IMG].reshape(N_DP, BIG_IMG)
    row_gain = jnp.take_along_axis(big_gain, big_seg, axis=1) * big_class.astype(jnp.float32)
    big_cot = (big_dout.reshape(N_DP, BIG_ROWS, features).astype(jnp.float32) + row_gain[:, :, None] * weight).astype(jnp.bfloat16)
    big_dq, big_dk, big_dv = lax.map(big_backward, (big_queries, big_keys, big_values, big_seg, big_cot.reshape(big_shape)))
    small_gain = image_gain[N_DP * BIG_IMG:]
    first_row = (slot_steps == 0).astype(jnp.float32)
    small_cot = owner_dout[slot_dest].reshape(groups, SMALL, features).astype(jnp.float32)
    small_cot = small_cot + small_gain[:, None, None] * first_row[None, :, None] * weight
    small_cot = small_cot.astype(jnp.bfloat16).reshape(groups, SMALL, HEADS, HD)
    small_dq, small_dk, small_dv = gradients(small_queries, small_keys, small_values, small_weights, small_cot)

    def to_rows(padded_grad):
        blank_rows = jnp.zeros((N_DP * MIG_ROWS, features), jnp.bfloat16)
        return blank_rows.at[scatter_at].set(padded_grad.reshape(-1, features), mode='drop')
    small_out = jnp.zeros((OWNER_ROWS, features), jnp.bfloat16).at[slot_dest].set(small_rows_out.reshape(-1, features))
    return (big_rows_out.reshape(BIG_TOTAL, features), small_out, big_dq.reshape(BIG_TOTAL, features), big_dk.reshape(BIG_TOTAL, features), big_dv.reshape(BIG_TOTAL, features), to_rows(small_dq), to_rows(small_dk), to_rows(small_dv), pair_loss)
```

```python
import functools
import math

import jax
import jax.numpy as jnp
from jax import lax
from jax.experimental import pallas as pl
from jax.experimental.pallas import tpu as pltpu
from jax.sharding import PartitionSpec as P

HD = 128
BIG_IMG = 4
MIG_IMG = 48
SMALL = 16
LANES = 128
IMAGES = BIG_IMG + MIG_IMG
SCALE = 1.0 / math.sqrt(HD)
EXP2_SCALE = SCALE * math.log2(math.e)
BLOCK = 128
WINDOW = 256
MASKED = -1e30


def mm(left, right):
    return jnp.dot(left, right, preferred_element_type=jnp.float32)


def mm_nt(left, right):
    return lax.dot_general(
        left, right, (((1,), (1,)), ((), ())), preferred_element_type=jnp.float32
    )


def mm_tn(left, right):
    return lax.dot_general(
        left, right, (((0,), (0,)), ((), ())), preferred_element_type=jnp.float32
    )


def iota(shape, dim):
    return lax.broadcasted_iota(jnp.int32, shape, dim)


def windows(rows):
    pairs = []
    for start in range(0, rows, BLOCK):
        pairs.append((start, min(max(start - (WINDOW - BLOCK) // 2, 0), rows - WINDOW)))
    return pairs


def image_ends(counts):
    first = counts[0]
    second = first + counts[1]
    third = second + counts[2]
    return first, second, third


def segment_of(rows, ends):
    return sum((rows >= end).astype(jnp.int32) for end in ends)


def class_mask_big(rows, counts):
    ends = image_ends(counts)
    lane = iota((rows, LANES), 1)
    start = jnp.where(
        lane == 0,
        0,
        jnp.where(
            lane == 1,
            ends[0],
            jnp.where(lane == 2, ends[1], jnp.where(lane == 3, ends[2], -1)),
        ),
    )
    return (iota((rows, LANES), 0) == start).astype(jnp.float32)


def small_tables(dev, image_ref, owner_ref):
    image = image_ref[pl.ds(lax.rem(dev, 8), 1), :]
    rows = image.shape[1]
    image_f = image.astype(jnp.float32)
    spread = jnp.broadcast_to(image_f, (LANES, rows))
    image_col = jnp.transpose(spread)
    before = jnp.zeros((1, rows), jnp.float32)
    for start in range(0, rows, LANES):
        column = image_col[start : start + LANES, 0:1]
        before = before + jnp.sum(
            (column < image_f).astype(jnp.float32), axis=0, keepdims=True
        )
    position = iota((1, rows), 1).astype(jnp.float32) - before
    owners = owner_ref[...].astype(jnp.float32)
    hot = iota((MIG_IMG, rows), 0) == image
    owner_row = jnp.sum(jnp.where(hot, owners, 0.0), axis=0, keepdims=True)
    dest = owner_row * SMALL + position
    sub = iota((LANES, rows), 0)
    stacked = jnp.where(sub == 0, image_f, jnp.where(sub == 1, position, dest))
    columns = jnp.transpose(stacked)
    return image, dest.astype(jnp.int32), columns


def class_mask_small(columns):
    lane = iota(columns.shape, 1)
    image = columns[:, 0:1].astype(jnp.int32)
    first = columns[:, 1:2] == 0.0
    return ((image + BIG_IMG == lane) & first).astype(jnp.float32)


def probs(queries, keys, allowed):
    scores = jnp.where(allowed, mm_nt(queries, keys), MASKED)
    top = jnp.max(scores, axis=-1, keepdims=True)
    grown = jnp.exp2((scores - top) * EXP2_SCALE)
    return (grown * (1.0 / jnp.sum(grown, axis=-1, keepdims=True))).astype(jnp.bfloat16)


def forward_kernel(
    dev_ref, counts_ref, bq, bk, bv, sq, sk, sv, image_ref, owner_ref, w_ref,
    big_out, slots_out, score_out,
    image_s, columns_s, place_s, big_class_s, small_class_s, rows_s,
):
    big_rows = bq.shape[0]
    small_rows = sq.shape[0]
    slot_rows = slots_out.shape[0]
    head = pl.program_id(0)
    ends = image_ends(counts_ref)

    @pl.when(head == 0)
    def _():
        image, dest, columns = small_tables(dev_ref[0], image_ref, owner_ref)
        image_s[...] = jnp.broadcast_to(image, image_s.shape)
        columns_s[...] = columns
        for start in range(0, slot_rows, BLOCK):
            place_s[start : start + BLOCK, :] = (
                (iota((BLOCK, small_rows), 0) + start == dest)
                .astype(jnp.float32)
                .astype(jnp.bfloat16)
            )
        big_class_s[...] = class_mask_big(big_rows, counts_ref)
        small_class_s[...] = class_mask_small(columns)
        score_out[...] = jnp.zeros_like(score_out)

    weight = w_ref[...]
    score = jnp.zeros((1, LANES), jnp.float32)
    for q0, k0 in windows(small_rows):
        image_col = columns_s[q0 : q0 + BLOCK, 0:1].astype(jnp.int32)
        allowed = image_col == image_s[0:1, k0 : k0 + WINDOW]
        weights = probs(sq[q0 : q0 + BLOCK, :], sk[k0 : k0 + WINDOW, :], allowed)
        out = mm(weights, sv[k0 : k0 + WINDOW, :]).astype(jnp.bfloat16)
        rows_s[q0 : q0 + BLOCK, :] = out
        dotted = jnp.sum(out.astype(jnp.float32) * weight, axis=1, keepdims=True)
        score = score + jnp.sum(
            dotted * small_class_s[q0 : q0 + BLOCK, :], axis=0, keepdims=True
        )
    placed = rows_s[...]
    for start in range(0, slot_rows, 256):
        slots_out[start : start + 256, :] = mm(place_s[start : start + 256, :], placed).astype(
            jnp.bfloat16
        )
    segment_row = segment_of(iota((1, big_rows), 1), ends)
    for q0 in range(0, big_rows, BLOCK):
        segment_col = segment_of(iota((BLOCK, 1), 0) + q0, ends)
        weights = probs(bq[q0 : q0 + BLOCK, :], bk[...], segment_col == segment_row)
        out = mm(weights, bv[...]).astype(jnp.bfloat16)
        big_out[q0 : q0 + BLOCK, :] = out
        dotted = jnp.sum(out.astype(jnp.float32) * weight, axis=1, keepdims=True)
        score = score + jnp.sum(
            dotted * big_class_s[q0 : q0 + BLOCK, :], axis=0, keepdims=True
        )
    score_out[...] += score


def pick(table, number, first_small):
    is_big = number < first_small
    small = number - first_small
    small_dev = (small * 21846) >> 20
    device = jnp.where(is_big, number >> 2, small_dev)
    lane = jnp.where(is_big, number & 3, BIG_IMG + small - MIG_IMG * small_dev)
    count = number.shape[1]
    chosen = (iota((table.shape[1], count), 0) == device).astype(jnp.float32)
    spread = jnp.dot(
        table,
        chosen,
        preferred_element_type=jnp.float32,
        precision=lax.Precision.HIGHEST,
    )
    return jnp.sum(
        jnp.where(iota(spread.shape, 0) == lane, spread, 0.0), axis=0, keepdims=True
    )


def backward_block(q, k, v, cot, allowed):
    weights = probs(q, k, allowed)
    wide = weights.astype(jnp.float32)
    weight_grad = mm_nt(cot, v)
    row_dot = jnp.sum(wide * weight_grad, axis=-1, keepdims=True)
    score_grad = (wide * (weight_grad - row_dot)).astype(jnp.bfloat16)
    return weights, score_grad


def backward_kernel(
    dev_ref, counts_ref, bq, bk, bv, bd, sq, sk, sv, sd, image_ref, owner_ref, w_ref,
    gathered_ref, pairs_ref,
    big_dq, big_dk, big_dv, small_dq, small_dk, small_dv, loss_out,
    image_s, columns_s, take_s, big_gain_s, small_gain_s, cot_s, dk_s, dv_s,
):
    big_rows = bq.shape[0]
    small_rows = sq.shape[0]
    slot_rows = sd.shape[0]
    head = pl.program_id(0)
    ends = image_ends(counts_ref)

    @pl.when(head == 0)
    def _():
        dev = dev_ref[0]
        image, _, columns = small_tables(dev, image_ref, owner_ref)
        image_s[...] = jnp.broadcast_to(image, image_s.shape)
        columns_s[...] = columns
        dest_col = columns[:, 2:3].astype(jnp.int32)
        for start in range(0, slot_rows, 256):
            take_s[:, start : start + 256] = (
                (iota((small_rows, 256), 1) + start == dest_col)
                .astype(jnp.float32)
                .astype(jnp.bfloat16)
            )
        first_small = gathered_ref.shape[0] * BIG_IMG
        table = jnp.transpose(gathered_ref[...])[0:56, :]
        preferred = pairs_ref[0:1, :]
        rejected = pairs_ref[1:2, :]
        margin = pick(table, rejected, first_small) - pick(table, preferred, first_small)
        small_exp = jnp.exp(-jnp.abs(margin))
        loss_out[...] = jnp.maximum(margin, 0.0) + jnp.log1p(small_exp)
        pull = jnp.where(margin >= 0, 1.0, small_exp) / (1.0 + small_exp)
        lane = iota((LANES, 1), 0)
        number = jnp.where(
            lane < BIG_IMG,
            dev * BIG_IMG + lane,
            jnp.where(lane < IMAGES, first_small + dev * MIG_IMG + lane - BIG_IMG, -1),
        )
        gain = jnp.sum(
            jnp.where(rejected == number, pull, 0.0)
            - jnp.where(preferred == number, pull, 0.0),
            axis=1,
            keepdims=True,
        )
        gain_row = jnp.transpose(jnp.broadcast_to(gain, (LANES, LANES)))[0:1, :]
        big_gain_s[...] = jnp.broadcast_to(
            jnp.sum(class_mask_big(big_rows, counts_ref) * gain_row, axis=1, keepdims=True),
            big_gain_s.shape,
        )
        small_gain_s[...] = jnp.broadcast_to(
            jnp.sum(class_mask_small(columns) * gain_row, axis=1, keepdims=True),
            small_gain_s.shape,
        )

    weight = w_ref[...]
    dk_s[...] = jnp.zeros_like(dk_s)
    dv_s[...] = jnp.zeros_like(dv_s)
    segment_row = segment_of(iota((1, big_rows), 1), ends)
    for q0 in range(0, big_rows, BLOCK):
        span = slice(q0, q0 + BLOCK)
        segment_col = segment_of(iota((BLOCK, 1), 0) + q0, ends)
        cot = (bd[span, :].astype(jnp.float32) + big_gain_s[span, :] * weight).astype(
            jnp.bfloat16
        )
        weights, score_grad = backward_block(
            bq[span, :], bk[...], bv[...], cot, segment_col == segment_row
        )
        big_dq[span, :] = (mm(score_grad, bk[...]) * SCALE).astype(jnp.bfloat16)
        dk_s[...] += mm_tn(score_grad, bq[span, :])
        dv_s[...] += mm_tn(weights, cot)
    big_dk[...] = (dk_s[...] * SCALE).astype(jnp.bfloat16)
    big_dv[...] = dv_s[...].astype(jnp.bfloat16)

    for start in range(0, small_rows, BLOCK):
        span = slice(start, start + BLOCK)
        cot_s[span, :] = (
            mm(take_s[span, :], sd[...]) + small_gain_s[span, :] * weight
        ).astype(jnp.bfloat16)
    small_span = slice(0, small_rows)
    dk_s[small_span, :] = jnp.zeros((small_rows, HD), jnp.float32)
    dv_s[small_span, :] = jnp.zeros((small_rows, HD), jnp.float32)
    for q0, k0 in windows(small_rows):
        span = slice(q0, q0 + BLOCK)
        keys = slice(k0, k0 + WINDOW)
        image_col = columns_s[span, 0:1].astype(jnp.int32)
        allowed = image_col == image_s[0:1, keys]
        cot = cot_s[span, :]
        weights, score_grad = backward_block(sq[span, :], sk[keys, :], sv[keys, :], cot, allowed)
        small_dq[span, :] = (mm(score_grad, sk[keys, :]) * SCALE).astype(jnp.bfloat16)
        dk_s[keys, :] += mm_tn(score_grad, sq[span, :])
        dv_s[keys, :] += mm_tn(weights, cot)
    small_dk[...] = (dk_s[small_span, :] * SCALE).astype(jnp.bfloat16)
    small_dv[...] = dv_s[small_span, :].astype(jnp.bfloat16)


def gather_scores(score):
    members = lax.axis_size("mp")
    step = 1
    while step < members:
        score = score + lax.ppermute(score, "mp", [(i, i ^ step) for i in range(members)])
        step *= 2
    devices = lax.axis_size("dp")
    index = lax.axis_index("dp")
    step = 1
    while step < devices:
        other = lax.ppermute(score, "dp", [(i, i ^ step) for i in range(devices)])
        upper = (index // step) % 2 == 1
        score = jnp.where(
            upper, jnp.concatenate([other, score]), jnp.concatenate([score, other])
        )
        step *= 2
    return score


def on_device(
    big_q, big_k, big_v, big_dout, big_counts, small_q, small_k, small_v,
    small_image, owner, owner_dout, reward_w, pair_perm,
):
    features = big_q.shape[1]
    heads = features // HD
    big_rows = big_q.shape[0]
    small_rows = small_q.shape[0]
    slot_rows = owner_dout.shape[0]
    bf16 = jnp.bfloat16
    dev = lax.axis_index("dp").astype(jnp.int32).reshape(1)
    counts = big_counts.reshape(-1)
    weight = reward_w.reshape(1, -1)
    pairs = pair_perm.reshape(-1, 2).T

    returned = lax.all_to_all(owner_dout, "dp", split_axis=0, concat_axis=0, tiled=True)

    def by_head(rows):
        return pl.BlockSpec((rows, HD), lambda h, d, c: (0, h))

    def whole(shape):
        return pl.BlockSpec(shape, lambda h, d, c: (0, 0))

    image_spec = pl.BlockSpec((8, small_rows), lambda h, d, c: (d[0] // 8, 0))
    owner_spec = pl.BlockSpec((MIG_IMG, 1), lambda h, d, c: (d[0], 0))
    big_flops = 2 * big_rows * big_rows * features
    small_flops = 2 * small_rows * WINDOW * features
    params = pltpu.CompilerParams(
        dimension_semantics=("arbitrary",), vmem_limit_bytes=56 * 2**20
    )

    big_out, slots, score = pl.pallas_call(
        forward_kernel,
        grid_spec=pltpu.PrefetchScalarGridSpec(
            num_scalar_prefetch=2,
            grid=(heads,),
            in_specs=[by_head(big_rows)] * 3
            + [by_head(small_rows)] * 3
            + [image_spec, owner_spec, by_head(1)],
            out_specs=[by_head(big_rows), by_head(slot_rows), whole((1, LANES))],
            scratch_shapes=[
                pltpu.VMEM((8, small_rows), jnp.int32),
                pltpu.VMEM((small_rows, LANES), jnp.float32),
                pltpu.VMEM((slot_rows, small_rows), bf16),
                pltpu.VMEM((big_rows, LANES), jnp.float32),
                pltpu.VMEM((small_rows, LANES), jnp.float32),
                pltpu.VMEM((small_rows, HD), bf16),
            ],
        ),
        out_shape=[
            jax.ShapeDtypeStruct((big_rows, features), bf16),
            jax.ShapeDtypeStruct((slot_rows, features), bf16),
            jax.ShapeDtypeStruct((1, LANES), jnp.float32),
        ],
        compiler_params=params,
        cost_estimate=pl.CostEstimate(
            flops=2 * big_flops + 2 * small_flops + 2 * slot_rows * small_rows * features,
            bytes_accessed=2 * features * (4 * big_rows + 3 * small_rows + slot_rows),
            transcendentals=heads * (big_rows * big_rows + small_rows * WINDOW),
        ),
    )(dev, counts, big_q, big_k, big_v, small_q, small_k, small_v, small_image, owner, weight)

    gathered = gather_scores(score)
    small_out = lax.all_to_all(slots, "dp", split_axis=0, concat_axis=0, tiled=True)

    pair_count = pairs.shape[1]
    grads = pl.pallas_call(
        backward_kernel,
        grid_spec=pltpu.PrefetchScalarGridSpec(
            num_scalar_prefetch=2,
            grid=(heads,),
            in_specs=[by_head(big_rows)] * 4
            + [by_head(small_rows)] * 3
            + [by_head(slot_rows), image_spec, owner_spec, by_head(1)]
            + [whole(gathered.shape), whole(pairs.shape)],
            out_specs=[by_head(big_rows)] * 3
            + [by_head(small_rows)] * 3
            + [whole((1, pair_count))],
            scratch_shapes=[
                pltpu.VMEM((8, small_rows), jnp.int32),
                pltpu.VMEM((small_rows, LANES), jnp.float32),
                pltpu.VMEM((small_rows, slot_rows), bf16),
                pltpu.VMEM((big_rows, LANES), jnp.float32),
                pltpu.VMEM((small_rows, LANES), jnp.float32),
                pltpu.VMEM((small_rows, HD), bf16),
                pltpu.VMEM((big_rows, HD), jnp.float32),
                pltpu.VMEM((big_rows, HD), jnp.float32),
            ],
        ),
        out_shape=[jax.ShapeDtypeStruct((big_rows, features), bf16)] * 3
        + [jax.ShapeDtypeStruct((small_rows, features), bf16)] * 3
        + [jax.ShapeDtypeStruct((1, pair_count), jnp.float32)],
        compiler_params=params,
        cost_estimate=pl.CostEstimate(
            flops=5 * big_flops + 5 * small_flops + 2 * slot_rows * small_rows * features,
            bytes_accessed=2 * features * (7 * big_rows + 6 * small_rows + slot_rows),
            transcendentals=heads * (big_rows * big_rows + small_rows * WINDOW),
        ),
    )(
        dev, counts, big_q, big_k, big_v, big_dout, small_q, small_k, small_v, returned,
        small_image, owner, weight, gathered, pairs,
    )
    big_dq, big_dk, big_dv, small_dq, small_dk, small_dv, loss = grads
    small_out, loss = lax.optimization_barrier((small_out, loss))
    return (
        big_out, small_out, big_dq, big_dk, big_dv, small_dq, small_dk, small_dv,
        loss.reshape(-1),
    )


def solution(mesh):
    rows = P("dp", "mp")
    return jax.shard_map(
        on_device,
        mesh=mesh,
        in_specs=(
            rows, rows, rows, rows, P("dp", None), rows, rows, rows, P(), P(), rows,
            P("mp"), P(),
        ),
        out_specs=(rows, rows, rows, rows, rows, rows, rows, rows, P()),
        check_vma=False,
    )
```

```python
import functools
import math

import jax
import jax.numpy as jnp
from jax import lax
from jax.experimental import pallas as pl
from jax.experimental.pallas import tpu as pltpu
from jax.sharding import PartitionSpec as P

HD = 128
BIG_IMG = 4
MIG_IMG = 48
SMALL = 16
LANES = 128
IMAGES = BIG_IMG + MIG_IMG
SCALE = 1.0 / math.sqrt(HD)
EXP2_SCALE = SCALE * math.log2(math.e)
BLOCK = 128
WINDOW = 256
MASKED = -1e30
X, Z = 4, 8


def mm(left, right):
    return jnp.dot(left, right, preferred_element_type=jnp.float32)


def mm_nt(left, right):
    return lax.dot_general(
        left, right, (((1,), (1,)), ((), ())), preferred_element_type=jnp.float32
    )


def mm_tn(left, right):
    return lax.dot_general(
        left, right, (((0,), (0,)), ((), ())), preferred_element_type=jnp.float32
    )


def iota(shape, dim):
    return lax.broadcasted_iota(jnp.int32, shape, dim)


def windows(rows):
    pairs = []
    for start in range(0, rows, BLOCK):
        pairs.append((start, min(max(start - (WINDOW - BLOCK) // 2, 0), rows - WINDOW)))
    return pairs


def image_ends(counts):
    first = counts[0]
    second = first + counts[1]
    third = second + counts[2]
    return first, second, third


def segment_of(rows, ends):
    return sum((rows >= end).astype(jnp.int32) for end in ends)


def class_mask_big(rows, counts):
    ends = image_ends(counts)
    lane = iota((rows, LANES), 1)
    start = jnp.where(
        lane == 0,
        0,
        jnp.where(
            lane == 1,
            ends[0],
            jnp.where(lane == 2, ends[1], jnp.where(lane == 3, ends[2], -1)),
        ),
    )
    return (iota((rows, LANES), 0) == start).astype(jnp.float32)


def small_tables(dev, image_ref, owner_ref):
    image = image_ref[pl.ds(lax.rem(dev, 8), 1), :]
    rows = image.shape[1]
    image_f = image.astype(jnp.float32)
    image_col = jnp.transpose(jnp.broadcast_to(image_f, (LANES, rows)))
    before = jnp.zeros((1, rows), jnp.float32)
    for start in range(0, rows, LANES):
        column = image_col[start : start + LANES, 0:1]
        before = before + jnp.sum(
            (column < image_f).astype(jnp.float32), axis=0, keepdims=True
        )
    position = iota((1, rows), 1).astype(jnp.float32) - before
    first = dev * MIG_IMG
    line = first // LANES
    last = owner_ref.shape[0] - 1
    lane = iota((LANES, LANES), 1)
    near = jnp.broadcast_to(owner_ref[pl.ds(line, 1), :], (LANES, LANES))
    far = jnp.broadcast_to(
        owner_ref[pl.ds(jnp.minimum(line + 1, last), 1), :], (LANES, LANES)
    )
    wanted = first - line * LANES + iota((LANES, LANES), 0)
    owners = jnp.sum(
        jnp.where(lane == wanted, near, 0) + jnp.where(lane + LANES == wanted, far, 0),
        axis=1,
        keepdims=True,
    )[0:MIG_IMG, :].astype(jnp.float32)
    hot = iota((MIG_IMG, rows), 0) == image
    owner_row = jnp.sum(jnp.where(hot, owners, 0.0), axis=0, keepdims=True)
    dest = owner_row * SMALL + position
    sub = iota((LANES, rows), 0)
    stacked = jnp.where(sub == 0, image_f, jnp.where(sub == 1, position, dest))
    columns = jnp.transpose(stacked)
    return image, dest.astype(jnp.int32), columns


def class_mask_small(columns):
    lane = iota(columns.shape, 1)
    image = columns[:, 0:1].astype(jnp.int32)
    first = columns[:, 1:2] == 0.0
    return ((image + BIG_IMG == lane) & first).astype(jnp.float32)


def probs(queries, keys, allowed):
    return softmax(mm_nt(queries, keys), allowed)


def softmax(products, allowed):
    scores = jnp.where(allowed, products, MASKED)
    top = jnp.max(scores, axis=-1, keepdims=True)
    grown = jnp.exp2((scores - top) * EXP2_SCALE)
    return (grown * (1.0 / jnp.sum(grown, axis=-1, keepdims=True))).astype(jnp.bfloat16)


def heads_of(ref):
    return [slice(start, start + HD) for start in range(0, ref.shape[1], HD)]


def score_kernel(dev_ref, counts_ref, bq, bk, bv, sq, sk, sv, image_ref, w_ref, score_out):
    big_rows = bq.shape[0]
    small_rows = sq.shape[0]
    ends = image_ends(counts_ref)
    heads = heads_of(bq)
    image = image_ref[pl.ds(lax.rem(dev_ref[0], 8), 1), :]
    number = iota((64, 1), 0)
    start = jnp.sum((image < number - BIG_IMG).astype(jnp.int32), axis=1, keepdims=True)
    chosen = (iota((64, small_rows), 1) == start).astype(jnp.float32).astype(jnp.bfloat16)
    big_number = iota((SMALL, 1), 0)
    big_start = jnp.where(
        big_number == 0,
        0,
        jnp.where(big_number == 1, ends[0], jnp.where(big_number == 2, ends[1], ends[2])),
    )
    big_chosen = (iota((SMALL, big_rows), 1) == big_start).astype(jnp.float32)
    small_q = mm(chosen, sq[...]).astype(jnp.bfloat16)
    big_q = mm(big_chosen.astype(jnp.bfloat16), bq[...]).astype(jnp.bfloat16)
    segment_row = segment_of(iota((1, big_rows), 1), ends)
    small_mask = image == number - BIG_IMG
    big_mask = jnp.minimum(big_number, BIG_IMG - 1) == segment_row
    small_products = [mm_nt(small_q[:, h], sk[:, h]) for h in heads]
    big_products = [mm_nt(big_q[:, h], bk[:, h]) for h in heads]
    small_weights = [softmax(products, small_mask) for products in small_products]
    big_weights = [softmax(products, big_mask) for products in big_products]
    small_out = [mm(weights, sv[:, h]) for weights, h in zip(small_weights, heads)]
    big_out = [mm(weights, bv[:, h]) for weights, h in zip(big_weights, heads)]

    def dotted(parts):
        total = sum(
            part.astype(jnp.bfloat16).astype(jnp.float32) * w_ref[:, h]
            for part, h in zip(parts, heads)
        )
        return jnp.sum(total, axis=1, keepdims=True)

    lane = iota((64, LANES), 1)
    is_small = (lane == number) & (number >= BIG_IMG) & (number < IMAGES)
    big_lane = iota((SMALL, LANES), 1)
    is_big = (big_lane == big_number) & (big_number < BIG_IMG)
    score_out[...] = jnp.sum(
        jnp.where(is_small, dotted(small_out), 0.0), axis=0, keepdims=True
    ) + jnp.sum(jnp.where(is_big, dotted(big_out), 0.0), axis=0, keepdims=True)


def small_allowed(image_s, columns_s, rows):
    parts = []
    for q0, k0 in windows(rows):
        image_col = columns_s[q0 : q0 + BLOCK, 0:1].astype(jnp.int32)
        parts.append(image_col == image_s[0:1, k0 : k0 + WINDOW])
    return jnp.concatenate(parts, axis=0)


def small_products(left, right):
    return jnp.concatenate(
        [
            mm_nt(left[q0 : q0 + BLOCK, :], right[k0 : k0 + WINDOW, :])
            for q0, k0 in windows(left.shape[0])
        ],
        axis=0,
    )


def small_sums(left, right):
    return jnp.concatenate(
        [
            mm(left[q0 : q0 + BLOCK, :], right[k0 : k0 + WINDOW, :])
            for q0, k0 in windows(left.shape[0])
        ],
        axis=0,
    )


def small_kernel(dev_ref, sq, sk, sv, image_ref, owner_ref, slots_out):
    small_rows = sq.shape[0]
    slot_rows = slots_out.shape[0]
    heads = heads_of(sq)
    image, dest, columns = small_tables(dev_ref[0], image_ref, owner_ref)
    allowed = small_allowed(image, columns, small_rows)
    products = [small_products(sq[:, h], sk[:, h]) for h in heads]
    weights = [softmax(product, allowed) for product in products]
    out = jnp.concatenate(
        [small_sums(weight, sv[:, h]).astype(jnp.bfloat16) for weight, h in zip(weights, heads)],
        axis=1,
    )
    for start in range(0, slot_rows, 256):
        place = (iota((256, small_rows), 0) + start == dest).astype(jnp.float32)
        slots_out[start : start + 256, :] = mm(place.astype(jnp.bfloat16), out).astype(
            jnp.bfloat16
        )


def pick(table, image, first_small, dev):
    is_big = image < first_small
    small = image - first_small
    small_dev = (small * 21846) >> 20
    device = jnp.where(is_big, image >> 2, small_dev)
    row = gathered_row(device, dev)
    lane = jnp.where(is_big, image & 3, BIG_IMG + small - MIG_IMG * small_dev)
    count = image.shape[1]
    chosen = (iota((table.shape[1], count), 0) == row).astype(jnp.float32)
    spread = jnp.dot(
        table,
        chosen,
        preferred_element_type=jnp.float32,
        precision=lax.Precision.HIGHEST,
    )
    return jnp.sum(
        jnp.where(iota(spread.shape, 0) == lane, spread, 0.0), axis=0, keepdims=True
    )


def score_gradient(weights, weight_grad):
    wide = weights.astype(jnp.float32)
    row_dot = jnp.sum(wide * weight_grad, axis=-1, keepdims=True)
    return (wide * (weight_grad - row_dot)).astype(jnp.bfloat16)


def backward_kernel(
    dev_ref, counts_ref, bq, bk, bv, bd, sq, sk, sv, sd, image_ref, owner_ref, w_ref,
    near_ref, far_ref, pairs_ref,
    big_out, big_dq, big_dk, big_dv, small_dq, small_dk, small_dv, loss_out,
    image_s, columns_s, take_s, big_gain_s, small_gain_s, dk_s, dv_s,
):
    big_rows = bq.shape[0]
    small_rows = sq.shape[0]
    slot_rows = sd.shape[0]
    head = pl.program_id(0)
    ends = image_ends(counts_ref)

    @pl.when(head == 0)
    def _():
        dev = dev_ref[0]
        image, _, columns = small_tables(dev, image_ref, owner_ref)
        image_s[...] = jnp.broadcast_to(image, image_s.shape)
        columns_s[...] = columns
        dest_col = columns[:, 2:3].astype(jnp.int32)
        for start in range(0, slot_rows, 256):
            take_s[:, start : start + 256] = (
                (iota((small_rows, 256), 1) + start == dest_col)
                .astype(jnp.float32)
                .astype(jnp.bfloat16)
            )
        first_small = X * Z * 2 * BIG_IMG
        table = jnp.concatenate([near_ref[...], far_ref[...]])
        table = jnp.transpose(table)[0:56, :]
        preferred = pairs_ref[0:1, :]
        rejected = pairs_ref[1:2, :]
        margin = pick(table, rejected, first_small, dev) - pick(
            table, preferred, first_small, dev
        )
        small_exp = jnp.exp(-jnp.abs(margin))
        loss_out[...] = jnp.maximum(margin, 0.0) + jnp.log1p(small_exp)
        pull = jnp.where(margin >= 0, 1.0, small_exp) / (1.0 + small_exp)
        lane = iota((LANES, 1), 0)
        number = jnp.where(
            lane < BIG_IMG,
            dev * BIG_IMG + lane,
            jnp.where(lane < IMAGES, first_small + dev * MIG_IMG + lane - BIG_IMG, -1),
        )
        gain = jnp.sum(
            jnp.where(rejected == number, pull, 0.0)
            - jnp.where(preferred == number, pull, 0.0),
            axis=1,
            keepdims=True,
        )
        gain_row = jnp.transpose(jnp.broadcast_to(gain, (LANES, LANES)))[0:1, :]
        big_gain_s[...] = jnp.broadcast_to(
            jnp.sum(class_mask_big(big_rows, counts_ref) * gain_row, axis=1, keepdims=True),
            big_gain_s.shape,
        )
        small_gain_s[...] = jnp.broadcast_to(
            jnp.sum(class_mask_small(columns) * gain_row, axis=1, keepdims=True),
            small_gain_s.shape,
        )

    weight = w_ref[...]
    segment_row = segment_of(iota((1, big_rows), 1), ends)
    segment_col = segment_of(iota((big_rows, 1), 0), ends)
    cot = (bd[...].astype(jnp.float32) + big_gain_s[...] * weight).astype(jnp.bfloat16)
    weights = probs(bq[...], bk[...], segment_col == segment_row)
    big_out[...] = mm(weights, bv[...]).astype(jnp.bfloat16)
    score_grad = score_gradient(weights, mm_nt(cot, bv[...]))
    big_dq[...] = (mm(score_grad, bk[...]) * SCALE).astype(jnp.bfloat16)
    big_dk[...] = (mm_tn(score_grad, bq[...]) * SCALE).astype(jnp.bfloat16)
    big_dv[...] = mm_tn(weights, cot).astype(jnp.bfloat16)

    cot = (mm(take_s[...], sd[...]) + small_gain_s[...] * weight).astype(jnp.bfloat16)
    allowed = small_allowed(image_s, columns_s, small_rows)
    weights = softmax(small_products(sq, sk), allowed)
    score_grad = score_gradient(weights, small_products(cot, sv))
    small_dq[...] = (small_sums(score_grad, sk) * SCALE).astype(jnp.bfloat16)
    dk_s[...] = jnp.zeros_like(dk_s)
    dv_s[...] = jnp.zeros_like(dv_s)
    for q0, k0 in windows(small_rows):
        span = slice(q0, q0 + BLOCK)
        keys = slice(k0, k0 + WINDOW)
        dk_s[keys, :] += mm_tn(score_grad[span, :], sq[span, :])
        dv_s[keys, :] += mm_tn(weights[span, :], cot[span, :])
    small_dk[...] = (dk_s[...] * SCALE).astype(jnp.bfloat16)
    small_dv[...] = dv_s[...].astype(jnp.bfloat16)


def sum_over_mp(score):
    members = lax.axis_size("mp")
    step = 1
    while step < members:
        score = score + lax.ppermute(score, "mp", [(i, i ^ step) for i in range(members)])
        step *= 2
    return score


def number(x, z, c):
    return (x % X * Z + z % Z) * 2 + c % 2


def fetch(score, distance):
    pairs = []
    for x in range(X):
        for z in range(Z):
            for c in range(2):
                dx, dz, dc = distance(x, z, c)
                pairs.append((number(x + dx, z + dz, c + dc), number(x, z, c)))
    return lax.ppermute(score, "dp", pairs)


def gather_core(score):
    other = fetch(score, lambda x, z, c: (0, 0, 1))
    return jnp.concatenate([score, other, jnp.zeros((6, LANES), score.dtype)])


def gather_z(rows):
    return jnp.concatenate(
        [fetch(rows[0:2], lambda x, z, c: (0, step + 3 * c, 0)) for step in (1, 2, 3, 4)]
    )


def gathered_row(device, dev):
    my_c, my_z, my_x = dev & 1, (dev >> 1) & (Z - 1), dev >> 4
    c, z, x = device & 1, (device >> 1) & (Z - 1), device >> 4
    dx, dz = (x - my_x) & (X - 1), (z - my_z) & (Z - 1)
    fetcher = jnp.where(dz > 4, 1, 0)
    block = jnp.where(fetcher == my_c, 8, 16)
    fetched = block + 2 * (dz - 1 - 3 * fetcher) + (c ^ fetcher)
    row = jnp.where(dz == 0, c ^ my_c, fetched)
    return ((dx & 1) * 2 + (dx >> 1)) * 24 + row


def by_head(rows):
    return pl.BlockSpec((rows, HD), lambda h, *_: (0, h))


def whole(shape):
    return pl.BlockSpec(shape, lambda h, *_: (0, 0))


def image_spec(small_rows):
    return pl.BlockSpec((8, small_rows), lambda h, d, *_: (d[0] // 8, 0))


PARAMS = pltpu.CompilerParams(
    dimension_semantics=("arbitrary",), vmem_limit_bytes=60 * 2**20
)


def score_call(
    dev, counts, big_q, big_k, big_v, small_q, small_k, small_v, small_image, weight
):
    big_rows, features = big_q.shape
    small_rows = small_q.shape[0]
    return pl.pallas_call(
        score_kernel,
        grid_spec=pltpu.PrefetchScalarGridSpec(
            num_scalar_prefetch=2,
            grid=(1,),
            in_specs=[whole(big_q.shape)] * 3
            + [whole(small_q.shape)] * 3
            + [image_spec(small_rows), whole(weight.shape)],
            out_specs=whole((1, LANES)),
        ),
        out_shape=jax.ShapeDtypeStruct((1, LANES), jnp.float32),
        compiler_params=PARAMS,
        cost_estimate=pl.CostEstimate(
            flops=6 * 64 * (small_rows + big_rows) * features,
            bytes_accessed=6 * features * (big_rows + small_rows),
            transcendentals=64 * 5 * (small_rows + big_rows),
        ),
    )(dev, counts, big_q, big_k, big_v, small_q, small_k, small_v, small_image, weight)


def small_call(dev, small_q, small_k, small_v, small_image, owner, slot_rows):
    small_rows, features = small_q.shape
    heads = features // HD
    return pl.pallas_call(
        small_kernel,
        grid_spec=pltpu.PrefetchScalarGridSpec(
            num_scalar_prefetch=1,
            grid=(1,),
            in_specs=[whole(small_q.shape)] * 3 + [image_spec(small_rows), whole(owner.shape)],
            out_specs=whole((slot_rows, features)),
        ),
        out_shape=jax.ShapeDtypeStruct((slot_rows, features), jnp.bfloat16),
        compiler_params=PARAMS,
        cost_estimate=pl.CostEstimate(
            flops=2 * slot_rows * small_rows * features + 4 * small_rows * WINDOW * features,
            bytes_accessed=2 * features * (3 * small_rows + slot_rows),
            transcendentals=heads * small_rows * WINDOW,
        ),
    )(dev, small_q, small_k, small_v, small_image, owner)


def backward_call(
    dev, counts, big_q, big_k, big_v, big_dout, small_q, small_k, small_v, returned,
    small_image, owner, weight, near, far, pairs,
):
    big_rows, features = big_q.shape
    small_rows = small_q.shape[0]
    slot_rows = returned.shape[0]
    heads = features // HD
    pair_count = pairs.shape[1]
    bf16 = jnp.bfloat16
    return pl.pallas_call(
        backward_kernel,
        grid_spec=pltpu.PrefetchScalarGridSpec(
            num_scalar_prefetch=2,
            grid=(heads,),
            in_specs=[by_head(big_rows)] * 4
            + [by_head(small_rows)] * 3
            + [by_head(slot_rows)]
            + [image_spec(small_rows), whole(owner.shape), by_head(1)]
            + [whole(near.shape), whole(far.shape), whole(pairs.shape)],
            out_specs=[by_head(big_rows)] * 4
            + [by_head(small_rows)] * 3
            + [whole((1, pair_count))],
            scratch_shapes=[
                pltpu.VMEM((8, small_rows), jnp.int32),
                pltpu.VMEM((small_rows, LANES), jnp.float32),
                pltpu.VMEM((small_rows, slot_rows), bf16),
                pltpu.VMEM((big_rows, LANES), jnp.float32),
                pltpu.VMEM((small_rows, LANES), jnp.float32),
                pltpu.VMEM((small_rows, HD), jnp.float32),
                pltpu.VMEM((small_rows, HD), jnp.float32),
            ],
        ),
        out_shape=[jax.ShapeDtypeStruct((big_rows, features), bf16)] * 4
        + [jax.ShapeDtypeStruct((small_rows, features), bf16)] * 3
        + [jax.ShapeDtypeStruct((1, pair_count), jnp.float32)],
        compiler_params=PARAMS,
        cost_estimate=pl.CostEstimate(
            flops=12 * big_rows * big_rows * features + 10 * small_rows * WINDOW * features,
            bytes_accessed=2 * features * (8 * big_rows + 6 * small_rows + slot_rows),
            transcendentals=heads * (big_rows * big_rows + small_rows * WINDOW),
        ),
    )(
        dev, counts, big_q, big_k, big_v, big_dout, small_q, small_k, small_v, returned,
        small_image, owner, weight, near, far, pairs,
    )


def on_device(
    big_q, big_k, big_v, big_dout, big_counts, small_q, small_k, small_v,
    small_image, owner, owner_dout, reward_w, pair_perm,
):
    dev = lax.axis_index("dp").astype(jnp.int32).reshape(1)
    counts = big_counts.reshape(-1)
    weight = reward_w.reshape(1, -1)
    pairs = pair_perm.reshape(-1, 2).T
    returned = lax.all_to_all(owner_dout, "dp", split_axis=0, concat_axis=0, tiled=True)
    owner = owner.reshape(-1, LANES)
    score = score_call(
        dev, counts, big_q, big_k, big_v, small_q, small_k, small_v, small_image, weight
    )
    slots = small_call(
        dev, small_q, small_k, small_v, small_image, owner, owner_dout.shape[0]
    )
    near = gather_core(sum_over_mp(score))
    fetched = gather_z(near)
    slots, fetched, returned, pairs = lax.optimization_barrier((slots, fetched, returned, pairs))
    near = jnp.concatenate([near, fetched, fetch(fetched, lambda x, z, c: (0, 0, 1))])
    slots, near = lax.optimization_barrier((slots, near))
    small_out = lax.all_to_all(slots, "dp", split_axis=0, concat_axis=0, tiled=True)
    near = jnp.concatenate([near, fetch(near, lambda x, z, c: (2, 0, 0))])
    far = fetch(near, lambda x, z, c: (1, 0, 0))
    big_out, big_dq, big_dk, big_dv, small_dq, small_dk, small_dv, loss = backward_call(
        dev, counts, big_q, big_k, big_v, big_dout, small_q, small_k, small_v, returned,
        small_image, owner, weight, near, far, pairs,
    )
    small_out, loss = lax.optimization_barrier((small_out, loss.reshape(-1)))
    return (
        big_out, small_out, big_dq, big_dk, big_dv, small_dq, small_dk, small_dv,
        loss,
    )


def solution(mesh):
    rows = P("dp", "mp")
    return jax.shard_map(
        on_device,
        mesh=mesh,
        in_specs=(
            rows, rows, rows, rows, P("dp", None), rows, rows, rows, P(), P(), rows,
            P("mp"), P(),
        ),
        out_specs=(rows, rows, rows, rows, rows, rows, rows, rows, P()),
        check_vma=False,
    )
```

```python
import functools
import math

import jax
import jax.numpy as jnp
from jax import lax
from jax.experimental import pallas as pl
from jax.experimental.pallas import tpu as pltpu
from jax.sharding import PartitionSpec as P

HD = 128
BIG_IMG = 4
MIG_IMG = 48
SMALL = 16
LANES = 128
IMAGES = BIG_IMG + MIG_IMG
SCALE = 1.0 / math.sqrt(HD)
EXP2_SCALE = SCALE * math.log2(math.e)
BLOCK = 128
WINDOW = 256
MASKED = -1e30
X, Z = 4, 8


def mm(left, right):
    return jnp.dot(left, right, preferred_element_type=jnp.float32)


def mm_nt(left, right):
    return lax.dot_general(
        left, right, (((1,), (1,)), ((), ())), preferred_element_type=jnp.float32
    )


def mm_tn(left, right):
    return lax.dot_general(
        left, right, (((0,), (0,)), ((), ())), preferred_element_type=jnp.float32
    )


def iota(shape, dim):
    return lax.broadcasted_iota(jnp.int32, shape, dim)


def windows(rows):
    pairs = []
    for start in range(0, rows, BLOCK):
        pairs.append((start, min(max(start - (WINDOW - BLOCK) // 2, 0), rows - WINDOW)))
    return pairs


def image_ends(counts):
    first = counts[0]
    second = first + counts[1]
    third = second + counts[2]
    return first, second, third


def segment_of(rows, ends):
    return sum((rows >= end).astype(jnp.int32) for end in ends)


def class_mask_big(rows, counts):
    ends = image_ends(counts)
    lane = iota((rows, LANES), 1)
    start = jnp.where(
        lane == 0,
        0,
        jnp.where(
            lane == 1,
            ends[0],
            jnp.where(lane == 2, ends[1], jnp.where(lane == 3, ends[2], -1)),
        ),
    )
    return (iota((rows, LANES), 0) == start).astype(jnp.float32)


def small_tables(dev, image_ref, owner_ref):
    image = image_ref[pl.ds(lax.rem(dev, 8), 1), :]
    rows = image.shape[1]
    image_f = image.astype(jnp.float32)
    image_col = jnp.transpose(jnp.broadcast_to(image_f, (LANES, rows)))
    before = jnp.zeros((1, rows), jnp.float32)
    for start in range(0, rows, LANES):
        column = image_col[start : start + LANES, 0:1]
        before = before + jnp.sum(
            (column < image_f).astype(jnp.float32), axis=0, keepdims=True
        )
    position = iota((1, rows), 1).astype(jnp.float32) - before
    first = dev * MIG_IMG
    line = first // LANES
    last = owner_ref.shape[0] - 1
    lane = iota((LANES, LANES), 1)
    near = jnp.broadcast_to(owner_ref[pl.ds(line, 1), :], (LANES, LANES))
    far = jnp.broadcast_to(
        owner_ref[pl.ds(jnp.minimum(line + 1, last), 1), :], (LANES, LANES)
    )
    wanted = first - line * LANES + iota((LANES, LANES), 0)
    owners = jnp.sum(
        jnp.where(lane == wanted, near, 0) + jnp.where(lane + LANES == wanted, far, 0),
        axis=1,
        keepdims=True,
    )[0:MIG_IMG, :].astype(jnp.float32)
    hot = iota((MIG_IMG, rows), 0) == image
    owner_row = jnp.sum(jnp.where(hot, owners, 0.0), axis=0, keepdims=True)
    dest = owner_row * SMALL + position
    sub = iota((LANES, rows), 0)
    stacked = jnp.where(sub == 0, image_f, jnp.where(sub == 1, position, dest))
    columns = jnp.transpose(stacked)
    return image, dest.astype(jnp.int32), columns


def class_mask_small(columns):
    lane = iota(columns.shape, 1)
    image = columns[:, 0:1].astype(jnp.int32)
    first = columns[:, 1:2] == 0.0
    return ((image + BIG_IMG == lane) & first).astype(jnp.float32)


def probs(queries, keys, allowed):
    return softmax(mm_nt(queries, keys), allowed)


def softmax(products, allowed):
    scores = jnp.where(allowed, products, MASKED)
    top = jnp.max(scores, axis=-1, keepdims=True)
    grown = jnp.exp2((scores - top) * EXP2_SCALE)
    return (grown * (1.0 / jnp.sum(grown, axis=-1, keepdims=True))).astype(jnp.bfloat16)


def heads_of(ref):
    return [slice(start, start + HD) for start in range(0, ref.shape[1], HD)]


def score_kernel(dev_ref, counts_ref, bq, bk, bv, sq, sk, sv, image_ref, w_ref, score_out):
    big_rows = bq.shape[0]
    small_rows = sq.shape[0]
    ends = image_ends(counts_ref)
    heads = heads_of(bq)
    image = image_ref[pl.ds(lax.rem(dev_ref[0], 8), 1), :]
    number = iota((64, 1), 0)
    start = jnp.sum((image < number - BIG_IMG).astype(jnp.int32), axis=1, keepdims=True)
    chosen = (iota((64, small_rows), 1) == start).astype(jnp.float32).astype(jnp.bfloat16)
    big_number = iota((SMALL, 1), 0)
    big_start = jnp.where(
        big_number == 0,
        0,
        jnp.where(big_number == 1, ends[0], jnp.where(big_number == 2, ends[1], ends[2])),
    )
    big_chosen = (iota((SMALL, big_rows), 1) == big_start).astype(jnp.float32)
    small_q = mm(chosen, sq[...]).astype(jnp.bfloat16)
    big_q = mm(big_chosen.astype(jnp.bfloat16), bq[...]).astype(jnp.bfloat16)
    segment_row = segment_of(iota((1, big_rows), 1), ends)
    small_mask = image == number - BIG_IMG
    big_mask = jnp.minimum(big_number, BIG_IMG - 1) == segment_row
    small_products = [mm_nt(small_q[:, h], sk[:, h]) for h in heads]
    big_products = [mm_nt(big_q[:, h], bk[:, h]) for h in heads]
    small_weights = [softmax(products, small_mask) for products in small_products]
    big_weights = [softmax(products, big_mask) for products in big_products]
    small_out = [mm(weights, sv[:, h]) for weights, h in zip(small_weights, heads)]
    big_out = [mm(weights, bv[:, h]) for weights, h in zip(big_weights, heads)]

    def dotted(parts):
        total = sum(
            part.astype(jnp.bfloat16).astype(jnp.float32) * w_ref[:, h]
            for part, h in zip(parts, heads)
        )
        return jnp.sum(total, axis=1, keepdims=True)

    lane = iota((64, LANES), 1)
    is_small = (lane == number) & (number >= BIG_IMG) & (number < IMAGES)
    big_lane = iota((SMALL, LANES), 1)
    is_big = (big_lane == big_number) & (big_number < BIG_IMG)
    score_out[...] = jnp.sum(
        jnp.where(is_small, dotted(small_out), 0.0), axis=0, keepdims=True
    ) + jnp.sum(jnp.where(is_big, dotted(big_out), 0.0), axis=0, keepdims=True)


def small_allowed(image_s, columns_s, rows):
    parts = []
    for q0, k0 in windows(rows):
        image_col = columns_s[q0 : q0 + BLOCK, 0:1].astype(jnp.int32)
        parts.append(image_col == image_s[0:1, k0 : k0 + WINDOW])
    return jnp.concatenate(parts, axis=0)


def small_products(left, right):
    return jnp.concatenate(
        [
            mm_nt(left[q0 : q0 + BLOCK, :], right[k0 : k0 + WINDOW, :])
            for q0, k0 in windows(left.shape[0])
        ],
        axis=0,
    )


def small_sums(left, right):
    return jnp.concatenate(
        [
            mm(left[q0 : q0 + BLOCK, :], right[k0 : k0 + WINDOW, :])
            for q0, k0 in windows(left.shape[0])
        ],
        axis=0,
    )


def small_kernel(dev_ref, sq, sk, sv, image_ref, owner_ref, slots_out):
    small_rows = sq.shape[0]
    slot_rows = slots_out.shape[0]
    heads = heads_of(sq)
    image, dest, columns = small_tables(dev_ref[0], image_ref, owner_ref)
    allowed = small_allowed(image, columns, small_rows)
    products = [small_products(sq[:, h], sk[:, h]) for h in heads]
    weights = [softmax(product, allowed) for product in products]
    out = jnp.concatenate(
        [small_sums(weight, sv[:, h]).astype(jnp.bfloat16) for weight, h in zip(weights, heads)],
        axis=1,
    )
    for start in range(0, slot_rows, 256):
        place = (iota((256, small_rows), 0) + start == dest).astype(jnp.float32)
        slots_out[start : start + 256, :] = mm(place.astype(jnp.bfloat16), out).astype(
            jnp.bfloat16
        )


def pick(table, image, first_small, dev):
    is_big = image < first_small
    small = image - first_small
    small_dev = (small * 21846) >> 20
    device = jnp.where(is_big, image >> 2, small_dev)
    row = gathered_row(device, dev)
    lane = jnp.where(is_big, image & 3, BIG_IMG + small - MIG_IMG * small_dev)
    count = image.shape[1]
    chosen = (iota((table.shape[1], count), 0) == row).astype(jnp.float32)
    spread = jnp.dot(
        table,
        chosen,
        preferred_element_type=jnp.float32,
        precision=lax.Precision.HIGHEST,
    )
    return jnp.sum(
        jnp.where(iota(spread.shape, 0) == lane, spread, 0.0), axis=0, keepdims=True
    )


def score_gradient(weights, weight_grad):
    wide = weights.astype(jnp.float32)
    row_dot = jnp.sum(wide * weight_grad, axis=-1, keepdims=True)
    return (wide * (weight_grad - row_dot)).astype(jnp.bfloat16)


def backward_kernel(
    dev_ref, counts_ref, bq, bk, bv, bd, sq, sk, sv, sd, image_ref, owner_ref, w_ref,
    near_ref, far_ref, pairs_ref,
    big_out, big_dq, big_dk, big_dv, small_dq, small_dk, small_dv, loss_out,
    image_s, columns_s, take_s, big_gain_s, small_gain_s, dk_s, dv_s,
):
    big_rows = bq.shape[0]
    small_rows = sq.shape[0]
    slot_rows = sd.shape[0]
    head = pl.program_id(0)
    ends = image_ends(counts_ref)

    @pl.when(head == 0)
    def _():
        dev = dev_ref[0]
        image, _, columns = small_tables(dev, image_ref, owner_ref)
        image_s[...] = jnp.broadcast_to(image, image_s.shape)
        columns_s[...] = columns
        dest_col = columns[:, 2:3].astype(jnp.int32)
        for start in range(0, slot_rows, 256):
            take_s[:, start : start + 256] = (
                (iota((small_rows, 256), 1) + start == dest_col)
                .astype(jnp.float32)
                .astype(jnp.bfloat16)
            )
        first_small = X * Z * 2 * BIG_IMG
        table = jnp.concatenate([near_ref[...], far_ref[...]])
        table = jnp.transpose(table)[0:56, :]
        images = pairs_ref[...]
        lines = images.shape[0]
        flat = jnp.concatenate([images[r : r + 1, :] for r in range(lines)], axis=1)
        scores = pick(table, flat, first_small, dev)
        scores = jnp.concatenate(
            [scores[:, r * LANES : (r + 1) * LANES] for r in range(lines)], axis=0
        )
        rejected = (iota(scores.shape, 1) & 1) == 1
        after = pltpu.roll(scores, LANES - 1, 1)
        before = pltpu.roll(scores, 1, 1)
        margin = jnp.where(rejected, scores - before, after - scores)
        small_exp = jnp.exp(-jnp.abs(margin))
        loss = jnp.maximum(margin, 0.0) + jnp.log1p(small_exp)
        pull = jnp.where(margin >= 0, 1.0, small_exp) / (1.0 + small_exp)
        signed = jnp.where(rejected, pull, -pull)
        source, target = iota((LANES, LANES), 0), iota((LANES, LANES), 1)
        half = LANES // 2

        def squeezed(offset):
            chosen = (source == 2 * (target - offset)) & (target >= offset)
            chosen = chosen & (target < offset + half)
            return jnp.dot(
                loss,
                chosen.astype(jnp.float32),
                preferred_element_type=jnp.float32,
                precision=lax.Precision.HIGHEST,
            )

        left, right = squeezed(0), squeezed(half)
        loss_out[...] = jnp.concatenate(
            [left[r : r + 1, :] + right[r + 1 : r + 2, :] for r in range(0, lines, 2)],
            axis=1,
        ).reshape(-1)
        lane = iota((64, 1), 0)
        number = jnp.where(
            lane < BIG_IMG,
            dev * BIG_IMG + lane,
            jnp.where(lane < IMAGES, first_small + dev * MIG_IMG + lane - BIG_IMG, -1),
        )
        gain = jnp.zeros((64, LANES), jnp.float32)
        for r in range(lines):
            gain = gain + jnp.where(images[r : r + 1, :] == number, signed[r : r + 1, :], 0.0)
        gain = jnp.sum(gain, axis=1, keepdims=True)
        gain = jnp.concatenate([gain, jnp.zeros_like(gain)], axis=0)
        gain_row = jnp.transpose(jnp.broadcast_to(gain, (LANES, LANES)))[0:1, :]
        big_gain_s[...] = jnp.broadcast_to(
            jnp.sum(class_mask_big(big_rows, counts_ref) * gain_row, axis=1, keepdims=True),
            big_gain_s.shape,
        )
        small_gain_s[...] = jnp.broadcast_to(
            jnp.sum(class_mask_small(columns) * gain_row, axis=1, keepdims=True),
            small_gain_s.shape,
        )

    weight = w_ref[...]
    segment_row = segment_of(iota((1, big_rows), 1), ends)
    segment_col = segment_of(iota((big_rows, 1), 0), ends)
    cot = (bd[...].astype(jnp.float32) + big_gain_s[...] * weight).astype(jnp.bfloat16)
    weights = probs(bq[...], bk[...], segment_col == segment_row)
    big_out[...] = mm(weights, bv[...]).astype(jnp.bfloat16)
    score_grad = score_gradient(weights, mm_nt(cot, bv[...]))
    big_dq[...] = (mm(score_grad, bk[...]) * SCALE).astype(jnp.bfloat16)
    big_dk[...] = (mm_tn(score_grad, bq[...]) * SCALE).astype(jnp.bfloat16)
    big_dv[...] = mm_tn(weights, cot).astype(jnp.bfloat16)

    cot = (mm(take_s[...], sd[...]) + small_gain_s[...] * weight).astype(jnp.bfloat16)
    allowed = small_allowed(image_s, columns_s, small_rows)
    weights = softmax(small_products(sq, sk), allowed)
    score_grad = score_gradient(weights, small_products(cot, sv))
    small_dq[...] = (small_sums(score_grad, sk) * SCALE).astype(jnp.bfloat16)
    dk_s[...] = jnp.zeros_like(dk_s)
    dv_s[...] = jnp.zeros_like(dv_s)
    for q0, k0 in windows(small_rows):
        span = slice(q0, q0 + BLOCK)
        keys = slice(k0, k0 + WINDOW)
        dk_s[keys, :] += mm_tn(score_grad[span, :], sq[span, :])
        dv_s[keys, :] += mm_tn(weights[span, :], cot[span, :])
    small_dk[...] = (dk_s[...] * SCALE).astype(jnp.bfloat16)
    small_dv[...] = dv_s[...].astype(jnp.bfloat16)


def sum_over_mp(score):
    members = lax.axis_size("mp")
    step = 1
    while step < members:
        score = score + lax.ppermute(score, "mp", [(i, i ^ step) for i in range(members)])
        step *= 2
    return score


def number(x, z, c):
    return (x % X * Z + z % Z) * 2 + c % 2


def fetch(score, distance):
    pairs = []
    for x in range(X):
        for z in range(Z):
            for c in range(2):
                dx, dz, dc = distance(x, z, c)
                pairs.append((number(x + dx, z + dz, c + dc), number(x, z, c)))
    return lax.ppermute(score, "dp", pairs)


def gather_core(score):
    other = fetch(score, lambda x, z, c: (0, 0, 1))
    return jnp.concatenate([score, other, jnp.zeros((6, LANES), score.dtype)])


def gather_z(rows):
    return jnp.concatenate(
        [fetch(rows[0:2], lambda x, z, c: (0, step + 3 * c, 0)) for step in (1, 2, 3, 4)]
    )


def gathered_row(device, dev):
    my_c, my_z, my_x = dev & 1, (dev >> 1) & (Z - 1), dev >> 4
    c, z, x = device & 1, (device >> 1) & (Z - 1), device >> 4
    dx, dz = (x - my_x) & (X - 1), (z - my_z) & (Z - 1)
    fetcher = jnp.where(dz > 4, 1, 0)
    block = jnp.where(fetcher == my_c, 8, 16)
    fetched = block + 2 * (dz - 1 - 3 * fetcher) + (c ^ fetcher)
    row = jnp.where(dz == 0, c ^ my_c, fetched)
    return ((dx & 1) * 2 + (dx >> 1)) * 24 + row


def by_head(rows):
    return pl.BlockSpec((rows, HD), lambda h, *_: (0, h))


def whole(shape):
    return pl.BlockSpec(shape, lambda h, *_: (0, 0))


def image_spec(small_rows):
    return pl.BlockSpec((8, small_rows), lambda h, d, *_: (d[0] // 8, 0))


def params(mebibytes):
    return pltpu.CompilerParams(
        dimension_semantics=("arbitrary",), vmem_limit_bytes=mebibytes * 2**20
    )


def score_call(
    dev, counts, big_q, big_k, big_v, small_q, small_k, small_v, small_image, weight
):
    big_rows, features = big_q.shape
    small_rows = small_q.shape[0]
    return pl.pallas_call(
        score_kernel,
        grid_spec=pltpu.PrefetchScalarGridSpec(
            num_scalar_prefetch=2,
            grid=(1,),
            in_specs=[whole(big_q.shape)] * 3
            + [whole(small_q.shape)] * 3
            + [image_spec(small_rows), whole(weight.shape)],
            out_specs=whole((1, LANES)),
        ),
        out_shape=jax.ShapeDtypeStruct((1, LANES), jnp.float32),
        compiler_params=params(63),
        cost_estimate=pl.CostEstimate(
            flops=6 * 64 * (small_rows + big_rows) * features,
            bytes_accessed=6 * features * (big_rows + small_rows),
            transcendentals=64 * 5 * (small_rows + big_rows),
        ),
    )(dev, counts, big_q, big_k, big_v, small_q, small_k, small_v, small_image, weight)


def small_call(dev, small_q, small_k, small_v, small_image, owner, slot_rows):
    small_rows, features = small_q.shape
    heads = features // HD
    return pl.pallas_call(
        small_kernel,
        grid_spec=pltpu.PrefetchScalarGridSpec(
            num_scalar_prefetch=1,
            grid=(1,),
            in_specs=[whole(small_q.shape)] * 3 + [image_spec(small_rows), whole(owner.shape)],
            out_specs=whole((slot_rows, features)),
        ),
        out_shape=jax.ShapeDtypeStruct((slot_rows, features), jnp.bfloat16),
        compiler_params=params(63),
        cost_estimate=pl.CostEstimate(
            flops=2 * slot_rows * small_rows * features + 4 * small_rows * WINDOW * features,
            bytes_accessed=2 * features * (3 * small_rows + slot_rows),
            transcendentals=heads * small_rows * WINDOW,
        ),
    )(dev, small_q, small_k, small_v, small_image, owner)


def backward_call(
    dev, counts, big_q, big_k, big_v, big_dout, small_q, small_k, small_v, returned,
    small_image, owner, weight, near, far, pairs,
):
    big_rows, features = big_q.shape
    small_rows = small_q.shape[0]
    slot_rows = returned.shape[0]
    heads = features // HD
    pair_count = pairs.size // 2
    bf16 = jnp.bfloat16
    return pl.pallas_call(
        backward_kernel,
        grid_spec=pltpu.PrefetchScalarGridSpec(
            num_scalar_prefetch=2,
            grid=(heads,),
            in_specs=[by_head(big_rows)] * 4
            + [by_head(small_rows)] * 3
            + [by_head(slot_rows)]
            + [image_spec(small_rows), whole(owner.shape), by_head(1)]
            + [whole(near.shape), whole(far.shape), whole(pairs.shape)],
            out_specs=[by_head(big_rows)] * 4
            + [by_head(small_rows)] * 3
            + [pl.BlockSpec((pair_count,), lambda h, *_: (0,))],
            scratch_shapes=[
                pltpu.VMEM((8, small_rows), jnp.int32),
                pltpu.VMEM((small_rows, LANES), jnp.float32),
                pltpu.VMEM((small_rows, slot_rows), bf16),
                pltpu.VMEM((big_rows, LANES), jnp.float32),
                pltpu.VMEM((small_rows, LANES), jnp.float32),
                pltpu.VMEM((small_rows, HD), jnp.float32),
                pltpu.VMEM((small_rows, HD), jnp.float32),
            ],
        ),
        out_shape=[jax.ShapeDtypeStruct((big_rows, features), bf16)] * 4
        + [jax.ShapeDtypeStruct((small_rows, features), bf16)] * 3
        + [jax.ShapeDtypeStruct((pair_count,), jnp.float32)],
        compiler_params=params(60),
        cost_estimate=pl.CostEstimate(
            flops=12 * big_rows * big_rows * features + 10 * small_rows * WINDOW * features,
            bytes_accessed=2 * features * (8 * big_rows + 6 * small_rows + slot_rows),
            transcendentals=heads * (big_rows * big_rows + small_rows * WINDOW),
        ),
    )(
        dev, counts, big_q, big_k, big_v, big_dout, small_q, small_k, small_v, returned,
        small_image, owner, weight, near, far, pairs,
    )


def on_device(
    big_q, big_k, big_v, big_dout, big_counts, small_q, small_k, small_v,
    small_image, owner, owner_dout, reward_w, pair_perm,
):
    dev = lax.axis_index("dp").astype(jnp.int32).reshape(1)
    counts = big_counts.reshape(-1)
    weight = reward_w.reshape(1, -1)
    pairs = pair_perm.reshape(-1, LANES)
    returned = lax.all_to_all(owner_dout, "dp", split_axis=0, concat_axis=0, tiled=True)
    owner = owner.reshape(-1, LANES)
    score = score_call(
        dev, counts, big_q, big_k, big_v, small_q, small_k, small_v, small_image, weight
    )
    slots = small_call(
        dev, small_q, small_k, small_v, small_image, owner, owner_dout.shape[0]
    )
    near = gather_core(sum_over_mp(score))
    fetched = gather_z(near)
    slots, fetched, returned = lax.optimization_barrier((slots, fetched, returned))
    small_out = lax.all_to_all(slots, "dp", split_axis=0, concat_axis=0, tiled=True)
    near = jnp.concatenate([near, fetched, fetch(fetched, lambda x, z, c: (0, 0, 1))])
    near = jnp.concatenate([near, fetch(near, lambda x, z, c: (2, 0, 0))])
    far = fetch(near, lambda x, z, c: (1, 0, 0))
    big_out, big_dq, big_dk, big_dv, small_dq, small_dk, small_dv, loss = backward_call(
        dev, counts, big_q, big_k, big_v, big_dout, small_q, small_k, small_v, returned,
        small_image, owner, weight, near, far, pairs,
    )
    small_out, loss = lax.optimization_barrier((small_out, loss))
    return (
        big_out, small_out, big_dq, big_dk, big_dv, small_dq, small_dk, small_dv,
        loss,
    )


def solution(mesh):
    rows = P("dp", "mp")
    return jax.shard_map(
        on_device,
        mesh=mesh,
        in_specs=(
            rows, rows, rows, rows, P("dp", None), rows, rows, rows, P(), P(), rows,
            P("mp"), P(),
        ),
        out_specs=(rows, rows, rows, rows, rows, rows, rows, rows, P()),
        check_vma=False,
    )
```
